128 devices in a mesh: dp: 16 (over x_lo, z, core), mp: 8 (over x_hi, y).
Axes of the slice: x: 4 (x_hi: 2, x_lo: 2; x = x_hi * 2 + x_lo), y: 4, z: 4, core: 2. Of those that a mesh axis runs over, the one named last changes fastest.
Arguments:
- tokens: bfloat16 [12288, 1024], P('dp', 'mp'), may hold values from -6 to 6
- segment_ids: int32 [12288], P('dp'), may hold values from 0 to 767, never falling along the last dimension, each value on 1 to 128 neighbouring positions
- mixer_gain: float32 [1024], P('mp'), may hold values from 0.1 to 1.9
- input_weight: bfloat16 [1024, 3, 1024], P('dp', None, 'mp'), may hold values from -0.1875 to 0.1875
- filter_weight: float32 [3, 1024], P(None, 'mp'), may hold values from -3.5 to 3.5
- output_weight: bfloat16 [1024, 1024], P('mp', 'dp'), may hold values from -0.1875 to 0.1875
- feed_gain: float32 [1024], P('mp'), may hold values from 0.1 to 1.9
- gate_weight: bfloat16 [1024, 4608], P('dp', 'mp'), may hold values from -0.1875 to 0.1875
- up_weight: bfloat16 [1024, 4608], P('dp', 'mp'), may hold values from -0.1875 to 0.1875
- down_weight: bfloat16 [4608, 1024], P('mp', 'dp'), may hold values from -0.09375 to 0.09375
- cotangent: bfloat16 [12288, 1024], P('dp', 'mp'), may hold values from -6 to 6
Outputs:
- block_out: bfloat16 [12288, 1024], P('dp', 'mp')
- input_grad: float32 [12288, 1024], P('dp', 'mp')
- mixer_gain_grad: float32 [1024], P('mp')
- input_weight_grad: float32 [1024, 3, 1024], P('dp', None, 'mp')
- filter_grad: float32 [3, 1024], P(None, 'mp')
- output_weight_grad: float32 [1024, 1024], P('mp', 'dp')
- feed_gain_grad: float32 [1024], P('mp')
- gate_weight_grad: float32 [1024, 4608], P('dp', 'mp')
- up_weight_grad: float32 [1024, 4608], P('dp', 'mp')
- down_weight_grad: float32 [4608, 1024], P('mp', 'dp')
The draws below stay inside these ranges and needn't reach their ends.
Inputs may be any that keep to these rules, and one draw needn't show every extreme that they name: `segment_ids`: segment numbers never fall along the tokens.
All inputs are finite; a program needn't handle non-finite values.
Results may differ from the reference program's by a relative error of at most 0.028.
Values may be sent and summed in bfloat16 or wider, within the bound.
No kernel may reach another device: no remote copies, remote signals or barrier semaphores. Data moves between devices by JAX's collectives and lax.ppermute only.
A program may use at most 64 MiB of HBM per device.

```python
import math
import jax
import jax.numpy as jnp
import numpy as np
from jax import lax

D = 1024
FF = 4608
SEQ_LEN = 768
TOKENS = 12288
N_DP = 16


def levels(key, shape, cuts, low, top_value):
    factor_of = 1.0
    for dim, blocks in cuts:
        draws = jax.random.uniform(jax.random.fold_in(jax.random.fold_in(key, 6), dim), (blocks,), jnp.float32, low / len(cuts), top_value / len(cuts))
        factor_of = factor_of * jnp.repeat(jnp.exp(draws), shape[dim] // blocks).reshape((-1,) + (1,) * (len(shape) - 1 - dim))
    return factor_of


def profile(amount, total, reach, slope):
    loads = [(1 << 20) // math.isqrt(grade ** slope) + 1 for grade in range(2, amount + 1)]
    spare, holding = total - reach - (amount - 1), [1] * (amount - 1)
    while spare > 0:
        candidates = [i for i in range(amount - 1) if holding[i] < reach]
        mass, left = sum([loads[i] for i in candidates]), spare
        for i in candidates:
            addition = min(reach - holding[i], max(1, left * loads[i] // mass), spare)
            holding[i] = holding[i] + addition
            spare = spare - addition
    return np.array([reach] + holding)


def uneven_parts(stream_key, count, total, limit, skew):
    if count == 2:
        one = jax.random.randint(stream_key, (), max(1, total - limit), min(limit, total - 1) + 1)
        return jnp.stack([one, total - one])
    sizes = jnp.asarray(profile(count, total, limit, skew), jnp.int32)
    pairs = (count - 1) // 2
    giver, receiver = sizes[1:1 + 2 * pairs:2], sizes[2:2 + 2 * pairs:2]
    room = jnp.minimum(giver - 1, limit - receiver)
    passed = jax.random.randint(jax.random.fold_in(stream_key, 1), (pairs,), 0, 1 << 20) % (room + 1)
    sizes = sizes.at[1:1 + 2 * pairs:2].set(giver - passed).at[2:2 + 2 * pairs:2].set(receiver + passed)
    return sizes[jax.random.permutation(jax.random.fold_in(stream_key, 2), count)]


def bell_draw(stream_key, extent, deviation, bound, shards=(), kind=jnp.bfloat16):
    loudness = levels(stream_key, extent, shards, -0.22, 0.18) if shards else 1.0
    array = jax.random.normal(stream_key, extent, jnp.float32) * deviation * loudness
    return jnp.minimum(jnp.maximum(array, -bound), bound).astype(kind)


def setup_inputs(seed: int = 0) -> dict:
    keys = jax.random.split(jax.random.key(seed), 12)
    tokens = bell_draw(keys[0], (TOKENS, D), 1.0, 6.0, ((0, 16), (1, 8)))
    segment_ids = jnp.searchsorted(jnp.cumsum(uneven_parts(keys[1], TOKENS // 16, TOKENS, min(128, SEQ_LEN), 2)), jnp.arange(TOKENS), side="right").astype(jnp.int32)
    mixer_gain = jnp.clip(1.0 + 0.18 * jax.random.normal(keys[2], (D,), jnp.float32), 0.1, 1.9)
    input_weight = bell_draw(keys[3], (D, 3, D), D ** -0.5, 0.1875, ((0, 16), (2, 8)))
    filter_weight = bell_draw(keys[4], (3, D), 3 ** -0.5, 3.5, ((1, 8),), jnp.float32)
    output_weight = bell_draw(keys[5], (D, D), D ** -0.5, 0.1875, ((0, 8), (1, 16)))
    feed_gain = jnp.clip(1.0 + 0.18 * jax.random.normal(keys[6], (D,), jnp.float32), 0.1, 1.9)
    gate_weight = bell_draw(keys[7], (D, FF), D ** -0.5, 0.1875, ((0, 16), (1, 8)))
    up_weight = bell_draw(keys[8], (D, FF), D ** -0.5, 0.1875, ((0, 16), (1, 8)))
    down_weight = bell_draw(keys[9], (FF, D), FF ** -0.5, 0.09375, ((0, 8), (1, 16)))
    cotangent = bell_draw(keys[10], (TOKENS, D), 1.0, 6.0, ((0, 16), (1, 8)))
    return dict(tokens=tokens, segment_ids=segment_ids, mixer_gain=mixer_gain, input_weight=input_weight, filter_weight=filter_weight, output_weight=output_weight, feed_gain=feed_gain, gate_weight=gate_weight, up_weight=up_weight, down_weight=down_weight, cotangent=cotangent)


@jax.custom_vjp
def low(v):
    return lax.optimization_barrier(v.astype(jnp.bfloat16)).astype(jnp.float32)

@jax.custom_vjp
def low_back(v):
    return v

def low_keep(v):
    return (low(v), None)

def low_pass(kept, grad):
    return (grad,)

def back_keep(v):
    return (v, None)

def back_low(kept, grad):
    return (low(grad),)
low.defvjp(low_keep, low_pass)
low_back.defvjp(back_keep, back_low)
eps = 1e-05

def norm_rows(values, gain):
    return values * lax.rsqrt(lax.optimization_barrier(jnp.mean(values * values, axis=1, keepdims=True)) + eps) * gain

def shift_down(values, steps):
    return jnp.concatenate([jnp.zeros((steps, values.shape[1]), values.dtype), values[:-steps]], axis=0)

def product(left, right):
    return jnp.dot(left, right, precision=lax.Precision.HIGHEST)

def block(seq_tokens, seq_segments, mixer_gain, input_weight, filter_weight, output_weight, feed_gain, gate_weight, up_weight, down_weight):
    features = seq_tokens.shape[1]
    positions = jnp.arange(seq_tokens.shape[0])
    first_in = low(norm_rows(seq_tokens, mixer_gain))
    projected = low_back(product(first_in, input_weight.reshape(features, 3 * features)))
    input_gate = projected[:, :features]
    output_gate = projected[:, features:2 * features]
    conv_input = projected[:, 2 * features:]
    mixed = input_gate * conv_input
    prev_one = jnp.concatenate([seq_segments[:1], seq_segments[:-1]])
    prev_two = jnp.concatenate([seq_segments[:2], seq_segments[:-2]])
    keep_one = jnp.where((positions >= 1) & (seq_segments == prev_one), 1.0, 0.0).astype(seq_tokens.dtype)[:, None]
    keep_two = jnp.where((positions >= 2) & (seq_segments == prev_two), 1.0, 0.0).astype(seq_tokens.dtype)[:, None]
    conv_out = filter_weight[2] * mixed + filter_weight[1] * shift_down(mixed, 1) * keep_one + filter_weight[0] * shift_down(mixed, 2) * keep_two
    gated = low(output_gate * conv_out)
    branch = low_back(product(gated, output_weight))
    resid = seq_tokens + branch
    second_in = low(norm_rows(resid, feed_gain))
    gate_value = low_back(product(second_in, gate_weight))
    up_value = low_back(product(second_in, up_weight))
    activated = low(jax.nn.silu(gate_value) * up_value)
    feed_out = low_back(product(activated, down_weight))
    return resid + feed_out

def reference(tokens, segment_ids, mixer_gain, input_weight, filter_weight, output_weight, feed_gain, gate_weight, up_weight, down_weight, cotangent):
    params = tuple((member.astype(jnp.float32) for member in (mixer_gain, input_weight, filter_weight, output_weight, feed_gain, gate_weight, up_weight, down_weight)))
    inputs = tokens.astype(jnp.float32).reshape(N_DP, SEQ_LEN, D)
    segments = segment_ids.reshape(N_DP, SEQ_LEN)
    upstream = cotangent.astype(jnp.float32).reshape(N_DP, SEQ_LEN, D)

    def visit(running, sliced):
        seq_tokens, seq_segments, seq_upstream = sliced

        def forward(seq_input, *weights):
            return block(seq_input, seq_segments, *weights)
        result, pullback = jax.vjp(forward, seq_tokens, *params)
        grads = pullback(seq_upstream)
        running = tuple((total + extra for total, extra in zip(running, grads[1:])))
        return (running, (result, grads[0]))
    zeros = tuple((jnp.zeros_like(member) for member in params))
    totals, (outputs, input_grads) = lax.scan(visit, zeros, (inputs, segments, upstream))
    block_out = outputs.reshape(TOKENS, D).astype(jnp.bfloat16)
    input_grad = input_grads.reshape(TOKENS, D)
    return (block_out, input_grad, totals[0], totals[1], totals[2], totals[3], totals[4], totals[5], totals[6], totals[7])
```

```python
import jax
import jax.numpy as jnp
from jax import lax
from jax.sharding import Mesh
from jax.sharding import PartitionSpec as P

eps = 1e-05
halo = 8
extra = 16
wide = ("xh", "dp")


def dot(left, right):
    return jnp.dot(left, right, preferred_element_type=jnp.float32)


def inner(left, right):
    return lax.dot_general(
        left, right, (((0,), (0,)), ((), ())), preferred_element_type=jnp.float32
    )


def against(left, right):
    return lax.dot_general(
        left, right, (((1,), (1,)), ((), ())), preferred_element_type=jnp.float32
    )


def swap(values, axis, mask):
    size = lax.axis_size(axis)
    return lax.ppermute(values, axis, [(i, i ^ mask) for i in range(size)])


def butterfly(items, bits):
    items = list(items)
    for level, bit in enumerate(bits):
        step = 1 << level
        items = [jnp.where(bit, items[k ^ step], items[k]) for k in range(len(items))]
    return items


def gather_y(values, bits):
    arrived = [values] + [swap(values, "y", k) for k in (1, 2, 3)]
    return butterfly(arrived, bits)


def natural(pairs):
    half = pairs[0].shape[1] // 2
    return jnp.concatenate([v[:, :half] for v in pairs] + [v[:, half:] for v in pairs], axis=1)


def scatter_y(values, bits):
    part = values.shape[1] // 8
    pairs = [
        jnp.concatenate(
            [
                values[:, p * part : (p + 1) * part],
                values[:, (4 + p) * part : (5 + p) * part],
            ],
            axis=1,
        )
        for p in range(4)
    ]
    mine = butterfly(pairs, bits)
    total = mine[0]
    for k in (1, 2, 3):
        total = total + swap(mine[k].astype(jnp.bfloat16), "y", k).astype(jnp.float32)
    return total


def devices(mask):
    return lambda values: swap(values, ("dp", "xh"), mask)


def gather_wide(values, xbits, zbits, core):
    rows, columns = values.shape
    along_z = butterfly([values] + [devices(m)(values) for m in (4, 8, 12)], zbits)
    along_z = jnp.stack(along_z)
    along_x = butterfly([along_z] + [devices(m)(along_z) for m in (16, 1, 17)], xbits)
    mine = jnp.stack(along_x)
    across = devices(2)(mine)
    both = jnp.stack(
        [jnp.where(core == 0, mine, across), jnp.where(core == 0, across, mine)], axis=2
    )
    return both.reshape(2, -1, columns)


def scatter_wide(parts, rows, xbits, zbits, core):
    columns = parts.shape[-1]
    bf16, f32 = jnp.bfloat16, jnp.float32
    parts = parts.reshape(4, 4, 2, rows, columns)
    first, second = parts[:, :, 0], parts[:, :, 1]
    send = jnp.where(core == 0, second, first).astype(bf16)
    held = jnp.where(core == 0, first, second) + devices(2)(send).astype(f32)
    held = butterfly([held[i] for i in range(4)], xbits)
    total = held[0]
    for k, m in enumerate((16, 1, 17)):
        total = total + devices(m)(held[k + 1].astype(bf16)).astype(f32)
    held = butterfly([total[i] for i in range(4)], zbits)
    total = held[0]
    for k, m in enumerate((4, 8, 12)):
        total = total + devices(m)(held[k + 1].astype(bf16)).astype(f32)
    return total


def sum_wide(values):
    for group in ((2,), (4, 8, 12), (1, 16, 17)):
        values = values + sum(swap(values, ("dp", "xh"), m) for m in group)
    return values


def split(values):
    high = lax.reduce_precision(values, 8, 7)
    return high.astype(jnp.bfloat16), (values - high).astype(jnp.bfloat16)


def windows(values, before, after):
    rows = values.shape[0] // 2
    padded = jnp.pad(values, ((before, after), (0, 0)))
    size = before + rows + after
    return padded[:size], padded[rows : rows + size]


def halves(own, got, h):
    return jnp.concatenate([jnp.where(h == 0, own, got), jnp.where(h == 0, got, own)], axis=1)


def to_columns(own, h):
    half = own.shape[1] // 2
    first, second = own[:, :half], own[:, half:]
    keep = jnp.where(h == 0, first, second)
    got = swap(jnp.where(h == 0, second, first), "xh", 1)
    return jnp.concatenate([jnp.where(h == 0, keep, got), jnp.where(h == 0, got, keep)], axis=0)


def body(
    tokens,
    segment_ids,
    mixer_gain,
    input_weight,
    filter_weight,
    output_weight,
    feed_gain,
    gate_weight,
    up_weight,
    down_weight,
    cotangent,
):
    h = lax.axis_index("xh")
    y = lax.axis_index("y")
    ybits = [(y & 1) == 1, (y & 2) == 2]
    place = lax.axis_index("dp")
    core = place & 1
    zbits = [(place & 2) == 2, (place & 4) == 4]
    xbits = [(place & 8) == 8, h == 1]
    length, channels = tokens.shape
    rows = length // 2
    owned_rows = input_weight.shape[0]
    features = owned_rows * lax.axis_size("dp")
    hidden = gate_weight.shape[1]
    padded_hidden = -(-hidden // 128) * 128
    lanes = ((0, 0), (0, padded_hidden - hidden))
    taps = filter_weight.shape[0]
    f32, bf16 = jnp.float32, jnp.bfloat16

    mix_local = jnp.concatenate(
        [input_weight.reshape(owned_rows, 3 * channels), output_weight.T], axis=1
    )
    feed_local = jnp.concatenate(
        [jnp.pad(w, lanes) for w in (gate_weight, up_weight, down_weight.T)], axis=1
    )
    feed_full = lax.all_gather(feed_local, wide, axis=0, tiled=True)
    mix_full = gather_wide(mix_local, xbits, zbits, core)
    w_in = [mix_full[s, :, : 3 * channels] for s in range(2)]
    w_out = jnp.concatenate([mix_full[s, :, 3 * channels :] for s in range(2)], axis=1)
    feed_full = feed_full.reshape(2, features, 3 * padded_hidden)
    w_up_gate = [feed_full[s, :, : 2 * padded_hidden] for s in range(2)]
    w_down = [feed_full[s, :, 2 * padded_hidden :] for s in range(2)]

    small = [split(v) for v in (mixer_gain, feed_gain)] + [split(filter_weight[i]) for i in range(taps)]
    small = jnp.stack([part for pair in small for part in pair])
    small = jnp.pad(small, ((0, extra - small.shape[0]), (0, 0)))
    first, second = windows(tokens, halo, halo)
    cot_first, cot_second = windows(cotangent, 0, halo)
    first = jnp.concatenate([small, first, cot_first], axis=0)
    second = jnp.concatenate([small, second, cot_second], axis=0)
    send = jnp.where(h == 0, second, first)
    pair = halves(jnp.where(h == 0, first, second), swap(send, "xh", 1), h)
    cot_at = extra + 2 * halo + rows
    tokens_pair, cot_pair = pair[:cot_at], pair[cot_at:]
    tokens_full = natural(gather_y(tokens_pair, ybits))
    cot_full = natural(gather_y(cot_pair, ybits))

    def joined(block, index):
        return block[2 * index].astype(f32) + block[2 * index + 1].astype(f32)

    small_full, tokens_full = tokens_full[:extra], tokens_full[extra:].astype(f32)
    small_own = tokens_pair[:extra]
    tokens_own = tokens_pair[extra + halo :].astype(f32)
    cot_own = cot_pair.astype(f32)
    mixer_full, feed_full_gain = joined(small_full, 0), joined(small_full, 1)
    mixer_own, feed_own = joined(small_own, 0), joined(small_own, 1)
    tap = [joined(small_own, 2 + i) for i in range(taps)]

    positions = jnp.arange(length)
    prev_one = jnp.concatenate([segment_ids[:1], segment_ids[:-1]])
    prev_two = jnp.concatenate([segment_ids[:2], segment_ids[:-2]])
    keep = jnp.stack(
        [
            jnp.where((positions >= 1) & (segment_ids == prev_one), 1.0, 0.0),
            jnp.where((positions >= 2) & (segment_ids == prev_two), 1.0, 0.0),
        ],
        axis=1,
    ).astype(f32)
    keep_first, keep_second = windows(keep, halo, halo)
    keep = jnp.where(h == 0, keep_first, keep_second)
    keep_one, keep_two = keep[:, :1], keep[:, 1:]

    inv_one = lax.rsqrt(jnp.mean(tokens_full * tokens_full, axis=1, keepdims=True) + eps)
    first_full = (tokens_full * inv_one * mixer_full).astype(bf16)
    projected = [dot(first_full, w) for w in w_in]

    def column(index):
        return jnp.concatenate(
            [p[:, index * channels : (index + 1) * channels] for p in projected], axis=1
        )

    input_gate, output_gate, conv_input = column(0), column(1), column(2)
    mixed = input_gate * conv_input
    pad_rows = jnp.zeros((2, mixed.shape[1]), f32)
    mixed_one = jnp.concatenate([pad_rows[:1], mixed[:-1]], axis=0) * keep_one
    mixed_two = jnp.concatenate([pad_rows, mixed[:-2]], axis=0) * keep_two
    conv_out = tap[2] * mixed + tap[1] * mixed_one + tap[0] * mixed_two
    late = slice(halo, None)
    gated = (output_gate[late] * conv_out[late]).astype(bf16)
    resid_own = tokens_own + scatter_y(against(gated, w_out), ybits)
    resid_send = resid_own.astype(bf16)
    resid_full = natural(gather_y(resid_send, ybits)).astype(f32)

    inv_two = lax.rsqrt(jnp.mean(resid_full * resid_full, axis=1, keepdims=True) + eps)
    normed_two = resid_full * inv_two
    second_full = (normed_two * feed_full_gain).astype(bf16)
    both = [dot(second_full, w) for w in w_up_gate]
    gate_value = [b[:, :padded_hidden] for b in both]
    up_value = [b[:, padded_hidden:] for b in both]
    gate_sigmoid = [jax.nn.sigmoid(g) for g in gate_value]
    activated = [(g * s * u).astype(bf16) for g, s, u in zip(gate_value, gate_sigmoid, up_value)]
    feed_out = sum(against(a[:rows], w) for a, w in zip(activated, w_down))
    block_own = (resid_own[:rows] + scatter_y(feed_out, ybits)).astype(bf16)
    block_out = to_columns(block_own, h)

    activated_grad = [dot(cot_full, w) for w in w_down]
    both_grad = [
        jnp.concatenate([d * u * s * (1.0 + g * (1.0 - s)), d * g * s], axis=1).astype(bf16)
        for d, g, u, s in zip(activated_grad, gate_value, up_value, gate_sigmoid)
    ]
    feed_wgrad = jnp.stack(
        [
            jnp.concatenate(
                [
                    inner(second_full[:rows], g[:rows]).astype(bf16),
                    inner(cot_full[:rows], a[:rows]).astype(bf16),
                ],
                axis=1,
            )
            for g, a in zip(both_grad, activated)
        ]
    )
    second_part = sum(against(g, w) for g, w in zip(both_grad, w_up_gate))
    second_send = scatter_y(second_part, ybits).astype(bf16)
    second_grad = natural(gather_y(second_send, ybits)).astype(f32)

    scaled = second_grad * feed_full_gain
    mean_two = jnp.mean(scaled * normed_two, axis=1, keepdims=True)
    resid_grad = cot_full.astype(f32) + inv_two * (scaled - normed_two * mean_two)
    second_own = second_send.astype(f32)
    normed_own = resid_send.astype(f32) * inv_two
    feed_gain_grad = jnp.sum((second_own * normed_own)[:rows], axis=0)
    resid_grad_own = cot_own + inv_two * (second_own * feed_own - normed_own * mean_two)

    resid_low = resid_grad.astype(bf16)
    output_wgrad = inner(resid_low[:rows], gated[:rows])
    gated_grad = dot(resid_low, w_out)
    conv_grad = gated_grad * output_gate[late]
    kept_one = conv_grad * keep_one[late]
    kept_two = conv_grad * keep_two[late]
    mixed_grad = (
        tap[2] * conv_grad[:rows]
        + tap[1] * kept_one[1 : rows + 1]
        + tap[0] * kept_two[2 : rows + 2]
    )
    inside = slice(halo, halo + rows)
    output_gate_grad = gated_grad[:rows] * conv_out[inside]
    conv_grad = conv_grad[:rows]
    filter_local = [
        jnp.sum(conv_grad * mixed_two[inside], axis=0),
        jnp.sum(conv_grad * mixed_one[inside], axis=0),
        jnp.sum(conv_grad * mixed[inside], axis=0),
    ]
    input_gate_grad = mixed_grad * conv_input[inside]
    conv_input_grad = mixed_grad * input_gate[inside]
    projected_grad = [
        jnp.concatenate(
            [
                v[:, s * channels : (s + 1) * channels]
                for v in (input_gate_grad, output_gate_grad, conv_input_grad)
            ],
            axis=1,
        ).astype(bf16)
        for s in range(2)
    ]
    row_sum = sum(
        jnp.sum(d.astype(f32) * p[inside], axis=1) for d, p in zip(projected_grad, projected)
    )
    row_sum = row_sum.reshape(rows // 128, 128)
    row_sum = row_sum + sum(swap(row_sum, "y", k) for k in (1, 2, 3))
    mean_one = row_sum.reshape(rows, 1) / features
    input_wgrad = [inner(first_full[inside], d) for d in projected_grad]
    first_own = scatter_y(sum(against(d, w) for d, w in zip(projected_grad, w_in)), ybits)
    normed_one = tokens_own[:rows] * inv_one[inside]
    mixer_gain_grad = jnp.sum(first_own * normed_one, axis=0)
    input_own = resid_grad_own[:rows] + inv_one[inside] * (
        first_own * mixer_own - normed_one * mean_one
    )
    input_grad = to_columns(input_own, h)

    feed_owned = lax.psum_scatter(
        feed_wgrad.reshape(2 * features, -1), wide, scatter_dimension=0, tiled=True
    ).astype(f32)
    gate_owned = feed_owned[:, :hidden]
    up_owned = feed_owned[:, padded_hidden : padded_hidden + hidden]
    down_owned = feed_owned[:, 2 * padded_hidden : 2 * padded_hidden + hidden].T
    mix_wgrad = jnp.stack(
        [
            jnp.concatenate([w, output_wgrad[:, s * channels : (s + 1) * channels]], axis=1)
            for s, w in enumerate(input_wgrad)
        ]
    )
    mix_owned = scatter_wide(mix_wgrad, owned_rows, xbits, zbits, core)
    input_owned = mix_owned[:, : 3 * channels].reshape(owned_rows, 3, channels)
    output_owned = mix_owned[:, 3 * channels :].T
    summed = sum_wide(jnp.stack([mixer_gain_grad, feed_gain_grad] + filter_local))
    summed = jnp.where(h == 0, summed[:, :channels], summed[:, channels:])
    return (
        block_out,
        input_grad,
        summed[0],
        input_owned,
        summed[2:],
        output_owned,
        summed[1],
        gate_owned,
        up_owned,
        down_owned,
    )


def solution(mesh):
    shape = mesh.devices.shape
    fine = Mesh(mesh.devices.reshape(shape[0], 2, shape[1] // 2), ("dp", "xh", "y"))
    mp = ("xh", "y")
    placed = (
        P("dp", mp),
        P("dp"),
        P(mp),
        P("dp", None, mp),
        P(None, mp),
        P(mp, "dp"),
        P(mp),
        P("dp", mp),
        P("dp", mp),
        P(mp, "dp"),
        P("dp", mp),
    )
    return jax.shard_map(
        body,
        mesh=fine,
        in_specs=placed,
        out_specs=(
            P("dp", mp),
            P("dp", mp),
            P(mp),
            P("dp", None, mp),
            P(None, mp),
            P(mp, "dp"),
            P(mp),
            P("dp", mp),
            P("dp", mp),
            P(mp, "dp"),
        ),
        check_vma=False,
    )
```

```python
import functools
import math

import jax
import jax.numpy as jnp
from jax import lax
from jax.experimental import pallas as pl
from jax.experimental.pallas import tpu as pltpu
from jax.sharding import Mesh
from jax.sharding import PartitionSpec as P

eps = 1e-05
halo = 8
extra = 16
wide = ("xh", "dp")
every = ("dp", "xh")


def dot(left, right):
    return jnp.dot(left, right, preferred_element_type=jnp.float32)


def inner(left, right):
    return lax.dot_general(
        left, right, (((0,), (0,)), ((), ())), preferred_element_type=jnp.float32
    )


def against(left, right):
    return lax.dot_general(
        left, right, (((1,), (1,)), ((), ())), preferred_element_type=jnp.float32
    )


def swap(values, axis, mask):
    size = lax.axis_size(axis)
    return lax.ppermute(values, axis, [(i, i ^ mask) for i in range(size)])


def butterfly(items, bits):
    items = list(items)
    for level, bit in enumerate(bits):
        step = 1 << level
        items = [jnp.where(bit, items[k ^ step], items[k]) for k in range(len(items))]
    return items


def gather_y(values, bits):
    arrived = [values] + [swap(values, "y", k) for k in (1, 2, 3)]
    return butterfly(arrived, bits)


def natural(pairs):
    half = pairs[0].shape[1] // 2
    return jnp.concatenate([v[:, :half] for v in pairs] + [v[:, half:] for v in pairs], axis=1)


def exchange_y(values, rider=None):
    rows, part = values.shape[0], values.shape[1] // 8
    sends = [
        jnp.concatenate(
            [
                values[:, p * part : (p + 1) * part],
                values[:, (4 + p) * part : (5 + p) * part],
            ],
            axis=1,
        ).astype(jnp.bfloat16)
        for p in range(4)
    ]
    if rider is not None:
        load = packed(rider, 2 * part)
        sends = [jnp.concatenate([v, load], axis=0) for v in sends]
    got = lax.all_to_all(jnp.stack(sends), "y", 0, 0)
    total = jnp.sum(got[:, :rows].astype(jnp.float32), axis=0)
    if rider is None:
        return total
    return total, sum(unpacked(got[i, rows:], rider.shape) for i in range(4))


def packed(values, columns):
    flat = values.reshape(-1)
    high, low = split(jnp.pad(flat, (0, -flat.size % columns)).reshape(-1, columns))
    both = jnp.concatenate([high, low], axis=0)
    return jnp.pad(both, ((0, -both.shape[0] % 16), (0, 0)))


def unpacked(block, shape):
    size = math.prod(shape)
    count = -(-size // block.shape[1])
    both = block[:count].astype(jnp.float32) + block[count : 2 * count].astype(jnp.float32)
    return both.reshape(-1)[:size].reshape(shape)


def scatter_y(values, bits):
    part = values.shape[1] // 8
    pairs = [
        jnp.concatenate(
            [
                values[:, p * part : (p + 1) * part],
                values[:, (4 + p) * part : (5 + p) * part],
            ],
            axis=1,
        )
        for p in range(4)
    ]
    mine = butterfly(pairs, bits)
    total = mine[0]
    for k in (1, 2, 3):
        total = total + swap(mine[k].astype(jnp.bfloat16), "y", k).astype(jnp.float32)
    return total


def devices(mask):
    return lambda values: swap(values, every, mask)


z_masks, x_masks, core_mask = (4, 8, 12), (16, 1, 17), 2


def gather_wide(values, xbits, zbits, core):
    columns = values.shape[1]
    along_x = jnp.stack(butterfly([values] + [devices(m)(values) for m in x_masks], xbits))
    along_z = butterfly([along_x] + [devices(m)(along_x) for m in z_masks], zbits)
    mine = jnp.stack(along_z, axis=1)
    across = devices(core_mask)(mine)
    both = jnp.stack(
        [jnp.where(core == 0, mine, across), jnp.where(core == 0, across, mine)], axis=2
    )
    return both.reshape(2, -1, columns)


def pick(values, index, axis):
    return lax.dynamic_index_in_dim(values, index, axis, keepdims=False)


def stage_sends(held, index, axis):
    sends = [pick(held, index ^ k, axis).astype(jnp.bfloat16) for k in (1, 2, 3)]
    return pick(held, index, axis).astype(jnp.float32), sends


def stage_arrive(sends, masks):
    return [devices(m)(v) for m, v in zip(masks, sends)]


def total_of(own, arrived):
    return own + sum(v.astype(jnp.float32) for v in arrived)


def ride(rider, masks):
    return rider + sum(devices(m)(rider) for m in masks)


def split(values):
    high = lax.reduce_precision(values, 8, 7)
    return high.astype(jnp.bfloat16), (values - high).astype(jnp.bfloat16)


def feed_kernel(rows, second, cot, grad0, grad1, act0, act1, out):
    width = out.shape[1]
    for s, (grad, act) in enumerate(((grad0, act0), (grad1, act1))):
        for j in range(3):

            @pl.when((pl.program_id(0) == s) & (pl.program_id(1) == j))
            def _():
                left = second if j < 2 else cot
                right = grad[:rows, j * width : (j + 1) * width] if j < 2 else act[:rows, :]
                out[...] = inner(left[:rows, :], right).astype(out.dtype)


def feed_wgrads(rows, second, cot, grads, acts):
    features, width = second.shape[1], acts[0].shape[1]
    operands = (second, cot, *grads, *acts)
    return pl.pallas_call(
        functools.partial(feed_kernel, rows),
        grid=(2, 3),
        in_specs=[pl.BlockSpec(v.shape, lambda s, j: (0, 0)) for v in operands],
        out_specs=pl.BlockSpec((features, width), lambda s, j: (s, j)),
        out_shape=pltpu.HBM((2 * features, 3 * width), jnp.bfloat16),
        compiler_params=pltpu.CompilerParams(vmem_limit_bytes=24 * 2**20),
        cost_estimate=pl.CostEstimate(
            flops=12 * rows * features * width,
            bytes_accessed=2 * sum(v.size for v in operands) + 12 * features * width,
            transcendentals=0,
        ),
    )(*operands)


def wgrad_kernel(rows, plan, summed, core, *refs):
    count = 2 if summed is None else 3
    operands, (send, held, *sums) = refs[:-count], refs[-count:]
    for s, line in enumerate(plan):
        for j, parts in enumerate(line):

            @pl.when((pl.program_id(0) == s) & (pl.program_id(1) == j))
            def _():
                at = 0
                for left, row, right, column, width in parts:
                    product = inner(
                        operands[left][row : row + rows, :],
                        operands[right][:rows, column : column + width],
                    )
                    if sums and at == 0:
                        terms = product * operands[summed + s][...].astype(jnp.float32)
                        terms = sum(terms[:, c : c + 128] for c in range(0, width, 128))
                        sums[0][...] = terms if s == 0 else sums[0][...] + terms
                    product = product.astype(send.dtype)
                    for b in range(8):
                        first = product[128 * b : 128 * b + 64]
                        second = product[128 * b + 64 : 128 * (b + 1)]
                        to = (slice(64 * b, 64 * (b + 1)), slice(at, at + width))
                        send[to] = jnp.where(core[0] == 0, second, first)
                        held[to] = jnp.where(core[0] == 0, first, second)
                    at += width


def wgrads(rows, plan, core, operands, summed=None, weight=1):
    features = operands[plan[0][0][0][0]].shape[1]
    width = sum(part[4] for part in plan[0][0])
    columns = width * len(plan[0])
    shape = jax.ShapeDtypeStruct((features, columns), jnp.bfloat16)
    block = pl.BlockSpec((features // 2, width), lambda s, j, c: (s, j))
    blocks, shapes = [block, block], [shape, shape]
    if summed is not None:
        blocks.append(pl.BlockSpec((features, 128), lambda s, j, c: (0, 0)))
        shapes.append(jax.ShapeDtypeStruct((features, 128), jnp.float32))
    return pl.pallas_call(
        functools.partial(wgrad_kernel, rows, plan, summed),
        grid_spec=pltpu.PrefetchScalarGridSpec(
            num_scalar_prefetch=1,
            grid=(2, len(plan[0])),
            in_specs=[pl.BlockSpec(v.shape, lambda s, j, c: (0, 0)) for v in operands],
            out_specs=blocks,
        ),
        out_shape=shapes,
        compiler_params=pltpu.CompilerParams(vmem_limit_bytes=24 * 2**20),
        cost_estimate=pl.CostEstimate(
            flops=weight * 4 * rows * features * columns,
            bytes_accessed=weight * (2 * sum(v.size for v in operands) + 4 * features * columns),
            transcendentals=0,
        ),
    )(core.reshape(1), *operands)


def windows(values, before, after):
    rows = values.shape[0] // 2
    padded = jnp.pad(values, ((before, after), (0, 0)))
    size = before + rows + after
    return padded[:size], padded[rows : rows + size]


def halves(own, got, h):
    return jnp.concatenate([jnp.where(h == 0, own, got), jnp.where(h == 0, got, own)], axis=1)


def body(
    tokens,
    segment_ids,
    mixer_gain,
    input_weight,
    filter_weight,
    output_weight,
    feed_gain,
    gate_weight,
    up_weight,
    down_weight,
    cotangent,
):
    h = lax.axis_index("xh")
    y = lax.axis_index("y")
    ybits = [(y & 1) == 1, (y & 2) == 2]
    place = lax.axis_index("dp")
    core = place & 1
    z = (place // 2) & 3
    x = place // 8 + 2 * h
    zbits = [(z & 1) == 1, (z & 2) == 2]
    xbits = [(x & 1) == 1, (x & 2) == 2]
    length, channels = tokens.shape
    rows = length // 2
    owned_rows = input_weight.shape[0]
    features = owned_rows * lax.axis_size("dp")
    hidden = gate_weight.shape[1]
    padded_hidden = -(-hidden // 128) * 128
    lanes = ((0, 0), (0, padded_hidden - hidden))
    taps = filter_weight.shape[0]
    f32, bf16 = jnp.float32, jnp.bfloat16

    mix_local = jnp.concatenate(
        [input_weight.reshape(owned_rows, 3 * channels), output_weight.T], axis=1
    )
    small = [split(v) for v in (mixer_gain, feed_gain)] + [split(filter_weight[i]) for i in range(taps)]
    small = jnp.stack([part for pair in small for part in pair])
    small = jnp.pad(small, ((0, extra - small.shape[0]), (0, 0)))
    first, second = windows(tokens, halo, halo)
    cot_first, cot_second = windows(cotangent, 0, halo)
    first = jnp.concatenate([small, first, cot_first], axis=0)
    second = jnp.concatenate([small, second, cot_second], axis=0)
    send = jnp.where(h == 0, second, first)
    own = jnp.where(h == 0, first, second)
    send, own, mix_local = lax.optimization_barrier((send, own, mix_local))
    gate_weight, send = lax.optimization_barrier((gate_weight, send))
    pair = halves(own, swap(send, "xh", 1), h)
    cot_at = extra + 2 * halo + rows
    tokens_pair, cot_pair = pair[:cot_at], pair[cot_at:]
    tokens_pair, cot_pair = pair[:cot_at], pair[cot_at:]
    tokens_full = natural(gather_y(tokens_pair, ybits))
    feed_local = jnp.concatenate(
        [jnp.pad(w, lanes) for w in (gate_weight, up_weight, down_weight.T)], axis=1
    )
    feed_full = lax.all_gather(feed_local, wide, axis=0, tiled=True)
    mix_full = gather_wide(mix_local, xbits, zbits, core)
    feed_full = feed_full.reshape(2, features, 3 * padded_hidden)
    w_up_gate = [feed_full[s, :, : 2 * padded_hidden] for s in range(2)]
    w_down = [feed_full[s, :, 2 * padded_hidden :] for s in range(2)]

    mix_full, cot_pair = lax.optimization_barrier((mix_full, cot_pair))
    cot_full = natural(gather_y(cot_pair, ybits))
    w_in = [mix_full[s, :, : 3 * channels] for s in range(2)]
    w_out = jnp.concatenate([mix_full[s, :, 3 * channels :] for s in range(2)], axis=1)

    def joined(block, index):
        return block[2 * index].astype(f32) + block[2 * index + 1].astype(f32)

    small_full, tokens_full = tokens_full[:extra], tokens_full[extra:].astype(f32)
    small_own = tokens_pair[:extra]
    tokens_own = tokens_pair[extra + halo :].astype(f32)
    cot_own = cot_pair.astype(f32)
    mixer_full, feed_full_gain = joined(small_full, 0), joined(small_full, 1)
    mixer_own, feed_own = joined(small_own, 0), joined(small_own, 1)
    tap = [joined(small_own, 2 + i) for i in range(taps)]

    positions = jnp.arange(length)
    prev_one = jnp.concatenate([segment_ids[:1], segment_ids[:-1]])
    prev_two = jnp.concatenate([segment_ids[:2], segment_ids[:-2]])
    keep = jnp.stack(
        [
            jnp.where((positions >= 1) & (segment_ids == prev_one), 1.0, 0.0),
            jnp.where((positions >= 2) & (segment_ids == prev_two), 1.0, 0.0),
        ],
        axis=1,
    ).astype(f32)
    keep_first, keep_second = windows(keep, halo, halo)
    keep = jnp.where(h == 0, keep_first, keep_second)
    keep_one, keep_two = keep[:, :1], keep[:, 1:]

    inv_one = lax.rsqrt(jnp.mean(tokens_full * tokens_full, axis=1, keepdims=True) + eps)
    first_full = (tokens_full * inv_one * mixer_full).astype(bf16)
    projected = [dot(first_full, w) for w in w_in]

    def column(index):
        return jnp.concatenate(
            [p[:, index * channels : (index + 1) * channels] for p in projected], axis=1
        )

    input_gate, output_gate, conv_input = column(0), column(1), column(2)
    mixed = input_gate * conv_input
    pad_rows = jnp.zeros((2, mixed.shape[1]), f32)
    mixed_one = jnp.concatenate([pad_rows[:1], mixed[:-1]], axis=0) * keep_one
    mixed_two = jnp.concatenate([pad_rows, mixed[:-2]], axis=0) * keep_two
    conv_out = tap[2] * mixed + tap[1] * mixed_one + tap[0] * mixed_two
    late = slice(halo, None)
    gated = (output_gate[late] * conv_out[late]).astype(bf16)
    resid_own = tokens_own + scatter_y(against(gated, w_out), ybits)
    resid_send = resid_own.astype(bf16)
    resid_full = natural(gather_y(resid_send, ybits)).astype(f32)

    inv_two = lax.rsqrt(jnp.mean(resid_full * resid_full, axis=1, keepdims=True) + eps)
    normed_two = resid_full * inv_two
    second_full = (normed_two * feed_full_gain).astype(bf16)
    both = [dot(second_full, w) for w in w_up_gate]
    gate_value = [b[:, :padded_hidden] for b in both]
    up_value = [b[:, padded_hidden:] for b in both]
    gate_sigmoid = [jax.nn.sigmoid(g) for g in gate_value]
    activated = [(g * s * u).astype(bf16) for g, s, u in zip(gate_value, gate_sigmoid, up_value)]
    feed_out = sum(against(a[:rows], w) for a, w in zip(activated, w_down))

    activated_grad = [dot(cot_full, w) for w in w_down]
    both_grad = [
        jnp.concatenate([d * u * s * (1.0 + g * (1.0 - s)), d * g * s], axis=1).astype(bf16)
        for d, g, u, s in zip(activated_grad, gate_value, up_value, gate_sigmoid)
    ]
    feed_wgrad = feed_wgrads(rows, second_full, cot_full, both_grad, activated)
    second_part = sum(against(g, w) for g, w in zip(both_grad, w_up_gate))
    second_send = scatter_y(second_part, ybits).astype(bf16)
    feed_owned = lax.psum_scatter(feed_wgrad, wide, scatter_dimension=0, tiled=True)
    second_grad = natural(gather_y(second_send, ybits))
    second_grad = second_grad.astype(f32)

    scaled = second_grad * feed_full_gain
    mean_two = jnp.mean(scaled * normed_two, axis=1, keepdims=True)
    resid_grad = cot_full.astype(f32) + inv_two * (scaled - normed_two * mean_two)
    second_own = second_send.astype(f32)
    normed_own = resid_send.astype(f32) * inv_two
    feed_gain_grad = jnp.sum((second_own * normed_own)[:rows], axis=0)
    resid_grad_own = cot_own + inv_two * (second_own * feed_own - normed_own * mean_two)

    resid_low = resid_grad.astype(bf16)
    gated_grad = dot(resid_low, w_out)
    conv_grad = gated_grad * output_gate[late]
    kept_one = conv_grad * keep_one[late]
    kept_two = conv_grad * keep_two[late]
    mixed_grad = (
        tap[2] * conv_grad[:rows]
        + tap[1] * kept_one[1 : rows + 1]
        + tap[0] * kept_two[2 : rows + 2]
    )
    inside = slice(halo, halo + rows)
    output_gate_grad = gated_grad[:rows] * conv_out[inside]
    conv_grad = conv_grad[:rows]
    filter_local = [
        jnp.sum(conv_grad * mixed_two[inside], axis=0),
        jnp.sum(conv_grad * mixed_one[inside], axis=0),
        jnp.sum(conv_grad * mixed[inside], axis=0),
    ]
    input_gate_grad = mixed_grad * conv_input[inside]
    conv_input_grad = mixed_grad * input_gate[inside]
    projected_grad = [
        jnp.concatenate(
            [
                v[:, s * channels : (s + 1) * channels]
                for v in (input_gate_grad, output_gate_grad, conv_input_grad)
            ],
            axis=1,
        ).astype(bf16)
        for s in range(2)
    ]
    row_sum = sum(
        jnp.sum(d.astype(f32) * p[inside], axis=1) for d, p in zip(projected_grad, projected)
    )
    plan = [
        [[(0, halo, 3 + t, 0, 3 * channels), (1, 0, 2, t * channels, channels)]]
        for t in range(2)
    ]
    mix_send, mix_held, gain_terms = wgrads(
        rows, plan, core, (first_full, resid_low, gated, *projected_grad, *w_in), 5, 40
    )
    mix_send, *projected_late = lax.optimization_barrier((mix_send, *projected_grad))
    mix_held = mix_held.astype(f32) + devices(core_mask)(mix_send).astype(f32)
    summed = jnp.concatenate([jnp.sum(gain_terms, axis=1) / mixer_full, feed_gain_grad, *filter_local])
    summed = ride(summed.reshape(-1, 2 * channels), (core_mask,))
    first_part = sum(against(d, w) for d, w in zip(projected_late, w_in))
    mix_own, sends = stage_sends(mix_held.reshape(4, 4, owned_rows, -1), x, 0)
    load = packed(summed, mix_own.shape[-1])
    sends = [jnp.concatenate([v.reshape(4 * owned_rows, -1), load], axis=0) for v in sends]
    first_part, mix_own, *sends = lax.optimization_barrier((first_part, mix_own, *sends))
    arrived = stage_arrive(sends, x_masks)
    late_own, row_sum = exchange_y(
        jnp.concatenate([first_part.astype(bf16), feed_out.astype(bf16)], axis=0),
        row_sum.reshape(-1, 128),
    )
    late_own, row_sum, *arrived = lax.optimization_barrier((late_own, row_sum, *arrived))
    first_own, block_own = late_own[:rows], resid_own[:rows] + late_own[rows:]
    mix_own = total_of(mix_own, [v[: 4 * owned_rows].reshape(mix_own.shape) for v in arrived])
    summed = total_of(summed, [unpacked(v[4 * owned_rows :], summed.shape) for v in arrived])
    mix_own, sends = stage_sends(mix_own, z, 0)
    load = packed(summed, mix_own.shape[1])
    arrived = stage_arrive([jnp.concatenate([v, load], axis=0) for v in sends], z_masks)
    mix_owned = total_of(mix_own, [v[:owned_rows] for v in arrived])
    summed = total_of(summed, [unpacked(v[owned_rows:], summed.shape) for v in arrived])
    gains = summed.reshape(-1, channels)
    place = 4 * h + y
    mixer_gain_grad = pick(gains, place, 0) + sum(
        swap(pick(gains, place ^ k, 0), "y", k) for k in (1, 2, 3)
    )
    summed = summed[4:]
    mean_one = row_sum.reshape(rows, 1) / features
    normed_one = tokens_own[:rows] * inv_one[inside]
    input_own = resid_grad_own[:rows] + inv_one[inside] * (
        first_own * mixer_own - normed_one * mean_one
    )
    half = jnp.concatenate([block_own, input_own], axis=0).astype(bf16)
    mine = jnp.where(h == 0, half[:, :channels], half[:, channels:])
    got = swap(jnp.where(h == 0, half[:, channels:], half[:, :channels]), "xh", 1)
    input_mine = jnp.where(h == 0, input_own[:, :channels], input_own[:, channels:])

    def ordered(own, other):
        return jnp.concatenate([jnp.where(h == 0, own, other), jnp.where(h == 0, other, own)], axis=0)

    block_out = ordered(mine[:rows], got[:rows])
    input_grad = ordered(input_mine, got[rows:].astype(f32))

    gate_owned, up_owned, down_owned = (
        feed_owned[:, t * padded_hidden : t * padded_hidden + hidden].astype(f32) for t in range(3)
    )
    down_owned = down_owned.T
    input_owned = mix_owned[:, : 3 * channels].reshape(owned_rows, 3, channels)
    output_owned = mix_owned[:, 3 * channels :].T
    summed = jnp.where(h == 0, summed[:, :channels], summed[:, channels:])
    return (
        block_out,
        input_grad,
        mixer_gain_grad,
        input_owned,
        summed[1:],
        output_owned,
        summed[0],
        gate_owned,
        up_owned,
        down_owned,
    )


def solution(mesh):
    shape = mesh.devices.shape
    fine = Mesh(mesh.devices.reshape(shape[0], 2, shape[1] // 2), ("dp", "xh", "y"))
    dp, mp = "dp", ("xh", "y")
    placed = (
        P(dp, mp),
        P(dp),
        P(mp),
        P(dp, None, mp),
        P(None, mp),
        P(mp, dp),
        P(mp),
        P(dp, mp),
        P(dp, mp),
        P(mp, dp),
        P(dp, mp),
    )
    return jax.shard_map(
        body,
        mesh=fine,
        in_specs=placed,
        out_specs=(
            P(dp, mp),
            P(dp, mp),
            P(mp),
            P(dp, None, mp),
            P(None, mp),
            P(mp, dp),
            P(mp),
            P(dp, mp),
            P(dp, mp),
            P(mp, dp),
        ),
        check_vma=False,
    )
```

```python
import functools
import math

import jax
import jax.numpy as jnp
from jax import lax
from jax.experimental import pallas as pl
from jax.experimental.pallas import tpu as pltpu
from jax.sharding import Mesh
from jax.sharding import PartitionSpec as P

eps = 1e-05
halo = 8
extra = 16
wide = ("xh", "dp")
every = ("dp", "xh")


def dot(left, right):
    return jnp.dot(left, right, preferred_element_type=jnp.float32)


def inner(left, right):
    return lax.dot_general(
        left, right, (((0,), (0,)), ((), ())), preferred_element_type=jnp.float32
    )


def against(left, right):
    return lax.dot_general(
        left, right, (((1,), (1,)), ((), ())), preferred_element_type=jnp.float32
    )


def swap(values, axis, mask):
    size = lax.axis_size(axis)
    return lax.ppermute(values, axis, [(i, i ^ mask) for i in range(size)])


def butterfly(items, bits):
    items = list(items)
    for level, bit in enumerate(bits):
        step = 1 << level
        items = [jnp.where(bit, items[k ^ step], items[k]) for k in range(len(items))]
    return items


def gather_y(values, bits):
    arrived = [values] + [swap(values, "y", k) for k in (1, 2, 3)]
    return butterfly(arrived, bits)


def natural(pairs):
    half = pairs[0].shape[1] // 2
    return jnp.concatenate([v[:, :half] for v in pairs] + [v[:, half:] for v in pairs], axis=1)


def exchange_y(values, bits, rider=None):
    rows, part = values.shape[0], values.shape[1] // 8
    sends = [
        jnp.concatenate(
            [
                values[:, p * part : (p + 1) * part],
                values[:, (4 + p) * part : (5 + p) * part],
            ],
            axis=1,
        ).astype(jnp.bfloat16)
        for p in range(4)
    ]
    if rider is not None:
        load = packed(rider, 2 * part)
        sends = [jnp.concatenate([v, load], axis=0) for v in sends]
    mine = butterfly(sends, bits)
    got = [mine[0]] + [swap(mine[k], "y", k) for k in (1, 2, 3)]
    total = sum(v[:rows].astype(jnp.float32) for v in got)
    if rider is None:
        return total
    return total, sum(unpacked(v[rows:], rider.shape) for v in got)


def packed(values, columns):
    flat = values.reshape(-1)
    high, low = split(jnp.pad(flat, (0, -flat.size % columns)).reshape(-1, columns))
    both = jnp.concatenate([high, low], axis=0)
    return jnp.pad(both, ((0, -both.shape[0] % 16), (0, 0)))


def unpacked(block, shape):
    size = math.prod(shape)
    count = -(-size // block.shape[1])
    both = block[:count].astype(jnp.float32) + block[count : 2 * count].astype(jnp.float32)
    return both.reshape(-1)[:size].reshape(shape)


def scatter_y(values, bits):
    part = values.shape[1] // 8
    pairs = [
        jnp.concatenate(
            [
                values[:, p * part : (p + 1) * part],
                values[:, (4 + p) * part : (5 + p) * part],
            ],
            axis=1,
        )
        for p in range(4)
    ]
    mine = butterfly(pairs, bits)
    total = mine[0]
    for k in (1, 2, 3):
        total = total + swap(mine[k].astype(jnp.bfloat16), "y", k).astype(jnp.float32)
    return total


def devices(mask):
    return lambda values: swap(values, every, mask)


z_masks, x_masks, core_mask = (4, 8, 12), (16, 1, 17), 2


def gather_wide(values, xbits, zbits, core):
    columns = values.shape[1]
    along_x = jnp.stack(butterfly([values] + [devices(m)(values) for m in x_masks], xbits))
    along_z = butterfly([along_x] + [devices(m)(along_x) for m in z_masks], zbits)
    mine = jnp.stack(along_z, axis=1)
    across = devices(core_mask)(mine)
    both = jnp.stack(
        [jnp.where(core == 0, mine, across), jnp.where(core == 0, across, mine)], axis=2
    )
    return both.reshape(2, -1, columns)


def pick(values, index, axis):
    return lax.dynamic_index_in_dim(values, index, axis, keepdims=False)


def stage_sends(held, index, axis):
    sends = [pick(held, index ^ k, axis).astype(jnp.bfloat16) for k in (1, 2, 3)]
    return pick(held, index, axis).astype(jnp.float32), sends


def stage_arrive(sends, masks):
    return [devices(m)(v) for m, v in zip(masks, sends)]


def total_of(own, arrived):
    return own + sum(v.astype(jnp.float32) for v in arrived)


def ride(rider, masks):
    return rider + sum(devices(m)(rider) for m in masks)


def split(values):
    high = lax.reduce_precision(values, 8, 7)
    return high.astype(jnp.bfloat16), (values - high).astype(jnp.bfloat16)


def feed_kernel(rows, second, cot, grad0, grad1, act0, act1, out):
    width = out.shape[1]
    for s, (grad, act) in enumerate(((grad0, act0), (grad1, act1))):
        for j in range(3):

            @pl.when((pl.program_id(0) == s) & (pl.program_id(1) == j))
            def _():
                left = second if j < 2 else cot
                right = grad[:rows, j * width : (j + 1) * width] if j < 2 else act[:rows, :]
                out[...] = inner(left[:rows, :], right).astype(out.dtype)


def feed_wgrads(rows, second, cot, grads, acts):
    features, width = second.shape[1], acts[0].shape[1]
    operands = (second, cot, *grads, *acts)
    return pl.pallas_call(
        functools.partial(feed_kernel, rows),
        grid=(2, 3),
        in_specs=[pl.BlockSpec(v.shape, lambda s, j: (0, 0)) for v in operands],
        out_specs=pl.BlockSpec((features, width), lambda s, j: (s, j)),
        out_shape=pltpu.HBM((2 * features, 3 * width), jnp.bfloat16),
        compiler_params=pltpu.CompilerParams(vmem_limit_bytes=24 * 2**20),
        cost_estimate=pl.CostEstimate(
            flops=12 * rows * features * width,
            bytes_accessed=2 * sum(v.size for v in operands) + 12 * features * width,
            transcendentals=0,
        ),
    )(*operands)


def wgrad_kernel(rows, plan, summed, core, *refs):
    count = 2 if summed is None else 3
    operands, (send, held, *sums) = refs[:-count], refs[-count:]
    for s, line in enumerate(plan):
        for j, parts in enumerate(line):

            @pl.when((pl.program_id(0) == s) & (pl.program_id(1) == j))
            def _():
                at = 0
                for left, row, right, column, width in parts:
                    product = inner(
                        operands[left][row : row + rows, :],
                        operands[right][:rows, column : column + width],
                    )
                    if sums and at == 0:
                        terms = product * operands[summed + s][...].astype(jnp.float32)
                        terms = sum(terms[:, c : c + 128] for c in range(0, width, 128))
                        sums[0][...] = terms if s == 0 else sums[0][...] + terms
                    product = product.astype(send.dtype)
                    for b in range(8):
                        first = product[128 * b : 128 * b + 64]
                        second = product[128 * b + 64 : 128 * (b + 1)]
                        to = (slice(64 * b, 64 * (b + 1)), slice(at, at + width))
                        send[to] = jnp.where(core[0] == 0, second, first)
                        held[to] = jnp.where(core[0] == 0, first, second)
                    at += width


def wgrads(rows, plan, core, operands, summed=None, weight=1):
    features = operands[plan[0][0][0][0]].shape[1]
    width = sum(part[4] for part in plan[0][0])
    columns = width * len(plan[0])
    shape = jax.ShapeDtypeStruct((features, columns), jnp.bfloat16)
    block = pl.BlockSpec((features // 2, width), lambda s, j, c: (s, j))
    blocks, shapes = [block, block], [shape, shape]
    if summed is not None:
        blocks.append(pl.BlockSpec((features, 128), lambda s, j, c: (0, 0)))
        shapes.append(jax.ShapeDtypeStruct((features, 128), jnp.float32))
    return pl.pallas_call(
        functools.partial(wgrad_kernel, rows, plan, summed),
        grid_spec=pltpu.PrefetchScalarGridSpec(
            num_scalar_prefetch=1,
            grid=(2, len(plan[0])),
            in_specs=[pl.BlockSpec(v.shape, lambda s, j, c: (0, 0)) for v in operands],
            out_specs=blocks,
        ),
        out_shape=shapes,
        compiler_params=pltpu.CompilerParams(vmem_limit_bytes=24 * 2**20),
        cost_estimate=pl.CostEstimate(
            flops=weight * 4 * rows * features * columns,
            bytes_accessed=weight * (2 * sum(v.size for v in operands) + 4 * features * columns),
            transcendentals=0,
        ),
    )(core.reshape(1), *operands)


def windows(values, before, after):
    rows = values.shape[0] // 2
    padded = jnp.pad(values, ((before, after), (0, 0)))
    size = before + rows + after
    return padded[:size], padded[rows : rows + size]


def halves(own, got, h):
    return jnp.concatenate([jnp.where(h == 0, own, got), jnp.where(h == 0, got, own)], axis=1)


def body(
    tokens,
    segment_ids,
    mixer_gain,
    input_weight,
    filter_weight,
    output_weight,
    feed_gain,
    gate_weight,
    up_weight,
    down_weight,
    cotangent,
):
    h = lax.axis_index("xh")
    y = lax.axis_index("y")
    ybits = [(y & 1) == 1, (y & 2) == 2]
    place = lax.axis_index("dp")
    core = place & 1
    z = (place // 2) & 3
    x = place // 8 + 2 * h
    zbits = [(z & 1) == 1, (z & 2) == 2]
    xbits = [(x & 1) == 1, (x & 2) == 2]
    length, channels = tokens.shape
    rows = length // 2
    owned_rows = input_weight.shape[0]
    features = owned_rows * lax.axis_size("dp")
    hidden = gate_weight.shape[1]
    padded_hidden = -(-hidden // 128) * 128
    lanes = ((0, 0), (0, padded_hidden - hidden))
    taps = filter_weight.shape[0]
    f32, bf16 = jnp.float32, jnp.bfloat16

    mix_local = jnp.concatenate(
        [input_weight.reshape(owned_rows, 3 * channels), output_weight.T], axis=1
    )
    small = [split(v) for v in (mixer_gain, feed_gain)] + [split(filter_weight[i]) for i in range(taps)]
    small = jnp.stack([part for pair in small for part in pair])
    small = jnp.pad(small, ((0, extra - small.shape[0]), (0, 0)))
    first, second = windows(tokens, halo, halo)
    cot_first, cot_second = windows(cotangent, 0, halo)
    first = jnp.concatenate([small, first, cot_first], axis=0)
    second = jnp.concatenate([small, second, cot_second], axis=0)
    send = jnp.where(h == 0, second, first)
    own = jnp.where(h == 0, first, second)
    send, own, mix_local = lax.optimization_barrier((send, own, mix_local))
    gate_weight, send = lax.optimization_barrier((gate_weight, send))
    pair = halves(own, swap(send, "xh", 1), h)
    cot_at = extra + 2 * halo + rows
    tokens_pair, cot_pair = pair[:cot_at], pair[cot_at:]
    tokens_pair, cot_pair = pair[:cot_at], pair[cot_at:]
    tokens_full = natural(gather_y(tokens_pair, ybits))
    feed_local = jnp.concatenate(
        [jnp.pad(w, lanes) for w in (gate_weight, up_weight, down_weight.T)], axis=1
    )
    feed_full = lax.all_gather(feed_local, wide, axis=0, tiled=True)
    mix_full = gather_wide(mix_local, xbits, zbits, core)
    feed_full = feed_full.reshape(2, features, 3 * padded_hidden)
    w_up_gate = [feed_full[s, :, : 2 * padded_hidden] for s in range(2)]
    w_down = [feed_full[s, :, 2 * padded_hidden :] for s in range(2)]

    mix_full, cot_pair = lax.optimization_barrier((mix_full, cot_pair))
    cot_full = natural(gather_y(cot_pair, ybits))
    w_in = [mix_full[s, :, : 3 * channels] for s in range(2)]
    w_out = jnp.concatenate([mix_full[s, :, 3 * channels :] for s in range(2)], axis=1)

    def joined(block, index):
        return block[2 * index].astype(f32) + block[2 * index + 1].astype(f32)

    small_full, tokens_full = tokens_full[:extra], tokens_full[extra:].astype(f32)
    small_own = tokens_pair[:extra]
    tokens_own = tokens_pair[extra + halo :].astype(f32)
    cot_own = cot_pair.astype(f32)
    mixer_full, feed_full_gain = joined(small_full, 0), joined(small_full, 1)
    mixer_own, feed_own = joined(small_own, 0), joined(small_own, 1)
    tap = [joined(small_own, 2 + i) for i in range(taps)]

    positions = jnp.arange(length)
    prev_one = jnp.concatenate([segment_ids[:1], segment_ids[:-1]])
    prev_two = jnp.concatenate([segment_ids[:2], segment_ids[:-2]])
    keep = jnp.stack(
        [
            jnp.where((positions >= 1) & (segment_ids == prev_one), 1.0, 0.0),
            jnp.where((positions >= 2) & (segment_ids == prev_two), 1.0, 0.0),
        ],
        axis=1,
    ).astype(f32)
    keep_first, keep_second = windows(keep, halo, halo)
    keep = jnp.where(h == 0, keep_first, keep_second)
    keep_one, keep_two = keep[:, :1], keep[:, 1:]

    inv_one = lax.rsqrt(jnp.mean(tokens_full * tokens_full, axis=1, keepdims=True) + eps)
    first_full = (tokens_full * inv_one * mixer_full).astype(bf16)
    projected = [dot(first_full, w) for w in w_in]

    def column(index):
        return jnp.concatenate(
            [p[:, index * channels : (index + 1) * channels] for p in projected], axis=1
        )

    input_gate, output_gate, conv_input = column(0), column(1), column(2)
    mixed = input_gate * conv_input
    pad_rows = jnp.zeros((2, mixed.shape[1]), f32)
    mixed_one = jnp.concatenate([pad_rows[:1], mixed[:-1]], axis=0) * keep_one
    mixed_two = jnp.concatenate([pad_rows, mixed[:-2]], axis=0) * keep_two
    conv_out = tap[2] * mixed + tap[1] * mixed_one + tap[0] * mixed_two
    late = slice(halo, None)
    gated = (output_gate[late] * conv_out[late]).astype(bf16)
    resid_own = tokens_own + scatter_y(against(gated, w_out), ybits)
    resid_send = resid_own.astype(bf16)
    resid_full = natural(gather_y(resid_send, ybits)).astype(f32)

    inv_two = lax.rsqrt(jnp.mean(resid_full * resid_full, axis=1, keepdims=True) + eps)
    normed_two = resid_full * inv_two
    second_full = (normed_two * feed_full_gain).astype(bf16)
    both = [dot(second_full, w) for w in w_up_gate]
    gate_value = [b[:, :padded_hidden] for b in both]
    up_value = [b[:, padded_hidden:] for b in both]
    gate_sigmoid = [jax.nn.sigmoid(g) for g in gate_value]
    activated = [(g * s * u).astype(bf16) for g, s, u in zip(gate_value, gate_sigmoid, up_value)]
    feed_out = sum(against(a[:rows], w) for a, w in zip(activated, w_down))

    activated_grad = [dot(cot_full, w) for w in w_down]
    both_grad = [
        jnp.concatenate([d * u * s * (1.0 + g * (1.0 - s)), d * g * s], axis=1).astype(bf16)
        for d, g, u, s in zip(activated_grad, gate_value, up_value, gate_sigmoid)
    ]
    feed_wgrad = feed_wgrads(rows, second_full, cot_full, both_grad, activated)
    second_part = sum(against(g, w) for g, w in zip(both_grad, w_up_gate))
    second_send = scatter_y(second_part, ybits).astype(bf16)
    feed_owned = lax.psum_scatter(feed_wgrad, wide, scatter_dimension=0, tiled=True)
    second_grad = natural(gather_y(second_send, ybits))
    second_grad = second_grad.astype(f32)

    scaled = second_grad * feed_full_gain
    mean_two = jnp.mean(scaled * normed_two, axis=1, keepdims=True)
    resid_grad = cot_full.astype(f32) + inv_two * (scaled - normed_two * mean_two)
    second_own = second_send.astype(f32)
    normed_own = resid_send.astype(f32) * inv_two
    feed_gain_grad = jnp.sum((second_own * normed_own)[:rows], axis=0)
    resid_grad_own = cot_own + inv_two * (second_own * feed_own - normed_own * mean_two)

    resid_low = resid_grad.astype(bf16)
    gated_grad = dot(resid_low, w_out)
    conv_grad = gated_grad * output_gate[late]
    kept_one = conv_grad * keep_one[late]
    kept_two = conv_grad * keep_two[late]
    mixed_grad = (
        tap[2] * conv_grad[:rows]
        + tap[1] * kept_one[1 : rows + 1]
        + tap[0] * kept_two[2 : rows + 2]
    )
    inside = slice(halo, halo + rows)
    output_gate_grad = gated_grad[:rows] * conv_out[inside]
    conv_grad = conv_grad[:rows]
    filter_local = [
        jnp.sum(conv_grad * mixed_two[inside], axis=0),
        jnp.sum(conv_grad * mixed_one[inside], axis=0),
        jnp.sum(conv_grad * mixed[inside], axis=0),
    ]
    input_gate_grad = mixed_grad * conv_input[inside]
    conv_input_grad = mixed_grad * input_gate[inside]
    projected_grad = [
        jnp.concatenate(
            [
                v[:, s * channels : (s + 1) * channels]
                for v in (input_gate_grad, output_gate_grad, conv_input_grad)
            ],
            axis=1,
        ).astype(bf16)
        for s in range(2)
    ]
    row_sum = sum(
        jnp.sum(d.astype(f32) * p[inside], axis=1) for d, p in zip(projected_grad, projected)
    )
    plan = [
        [[(0, halo, 3 + t, 0, 3 * channels), (1, 0, 2, t * channels, channels)]]
        for t in range(2)
    ]
    mix_send, mix_held, gain_terms = wgrads(
        rows, plan, core, (first_full, resid_low, gated, *projected_grad, *w_in), 5, 40
    )
    mix_send, *projected_late = lax.optimization_barrier((mix_send, *projected_grad))
    mix_held = mix_held.astype(f32) + devices(core_mask)(mix_send).astype(f32)
    summed = jnp.concatenate([jnp.sum(gain_terms, axis=1) / mixer_full, feed_gain_grad, *filter_local])
    summed = ride(summed.reshape(-1, 2 * channels), (core_mask,))
    first_part = sum(against(d, w) for d, w in zip(projected_late, w_in))
    mix_own, sends = stage_sends(mix_held.reshape(4, 4, owned_rows, -1), x, 0)
    load = packed(summed, mix_own.shape[-1])
    sends = [jnp.concatenate([v.reshape(4 * owned_rows, -1), load], axis=0) for v in sends]
    first_part, mix_own, *sends = lax.optimization_barrier((first_part, mix_own, *sends))
    arrived = stage_arrive(sends, x_masks)
    late_own, row_sum = exchange_y(
        jnp.concatenate([first_part.astype(bf16), feed_out.astype(bf16)], axis=0),
        ybits,
        row_sum.reshape(-1, 128),
    )
    late_own, row_sum, *arrived = lax.optimization_barrier((late_own, row_sum, *arrived))
    first_own, block_own = late_own[:rows], resid_own[:rows] + late_own[rows:]
    mix_own = total_of(mix_own, [v[: 4 * owned_rows].reshape(mix_own.shape) for v in arrived])
    summed = total_of(summed, [unpacked(v[4 * owned_rows :], summed.shape) for v in arrived])
    mix_own, sends = stage_sends(mix_own, z, 0)
    load = packed(summed, mix_own.shape[1])
    arrived = stage_arrive([jnp.concatenate([v, load], axis=0) for v in sends], z_masks)
    mix_owned = total_of(mix_own, [v[:owned_rows] for v in arrived])
    summed = total_of(summed, [unpacked(v[owned_rows:], summed.shape) for v in arrived])
    gains = summed.reshape(-1, channels)
    place = 4 * h + y
    mixer_gain_grad = pick(gains, place, 0) + sum(
        swap(pick(gains, place ^ k, 0), "y", k) for k in (1, 2, 3)
    )
    summed = summed[4:]
    mean_one = row_sum.reshape(rows, 1) / features
    normed_one = tokens_own[:rows] * inv_one[inside]
    input_own = resid_grad_own[:rows] + inv_one[inside] * (
        first_own * mixer_own - normed_one * mean_one
    )
    half = jnp.concatenate([block_own, input_own], axis=0).astype(bf16)
    mine = jnp.where(h == 0, half[:, :channels], half[:, channels:])
    got = swap(jnp.where(h == 0, half[:, channels:], half[:, :channels]), "xh", 1)
    input_mine = jnp.where(h == 0, input_own[:, :channels], input_own[:, channels:])

    def ordered(own, other):
        return jnp.concatenate([jnp.where(h == 0, own, other), jnp.where(h == 0, other, own)], axis=0)

    block_out = ordered(mine[:rows], got[:rows])
    input_grad = ordered(input_mine, got[rows:].astype(f32))

    gate_owned, up_owned, down_owned = (
        feed_owned[:, t * padded_hidden : t * padded_hidden + hidden].astype(f32) for t in range(3)
    )
    down_owned = down_owned.T
    input_owned = mix_owned[:, : 3 * channels].reshape(owned_rows, 3, channels)
    output_owned = mix_owned[:, 3 * channels :].T
    summed = jnp.where(h == 0, summed[:, :channels], summed[:, channels:])
    return (
        block_out,
        input_grad,
        mixer_gain_grad,
        input_owned,
        summed[1:],
        output_owned,
        summed[0],
        gate_owned,
        up_owned,
        down_owned,
    )


def solution(mesh):
    shape = mesh.devices.shape
    fine = Mesh(mesh.devices.reshape(shape[0], 2, shape[1] // 2), ("dp", "xh", "y"))
    dp, mp = "dp", ("xh", "y")
    placed = (
        P(dp, mp),
        P(dp),
        P(mp),
        P(dp, None, mp),
        P(None, mp),
        P(mp, dp),
        P(mp),
        P(dp, mp),
        P(dp, mp),
        P(mp, dp),
        P(dp, mp),
    )
    return jax.shard_map(
        body,
        mesh=fine,
        in_specs=placed,
        out_specs=(
            P(dp, mp),
            P(dp, mp),
            P(mp),
            P(dp, None, mp),
            P(None, mp),
            P(mp, dp),
            P(mp),
            P(dp, mp),
            P(dp, mp),
            P(mp, dp),
        ),
        check_vma=False,
    )
```

```python
import functools
import math

import jax
import jax.numpy as jnp
from jax import lax
from jax.experimental import pallas as pl
from jax.experimental.pallas import tpu as pltpu
from jax.sharding import Mesh
from jax.sharding import PartitionSpec as P

eps = 1e-05
halo = 8
extra = 16
wide = ("xh", "dp")
every = ("dp", "xh")


def dot(left, right):
    return jnp.dot(left, right, preferred_element_type=jnp.float32)


def inner(left, right):
    return lax.dot_general(
        left, right, (((0,), (0,)), ((), ())), preferred_element_type=jnp.float32
    )


def against(left, right):
    return lax.dot_general(
        left, right, (((1,), (1,)), ((), ())), preferred_element_type=jnp.float32
    )


def swap(values, axis, mask):
    size = lax.axis_size(axis)
    return lax.ppermute(values, axis, [(i, i ^ mask) for i in range(size)])


def butterfly(items, bits):
    items = list(items)
    for level, bit in enumerate(bits):
        step = 1 << level
        items = [jnp.where(bit, items[k ^ step], items[k]) for k in range(len(items))]
    return items


def gather_y(values, bits):
    arrived = [values] + [swap(values, "y", k) for k in (1, 2, 3)]
    return butterfly(arrived, bits)


def natural(pairs):
    half = pairs[0].shape[1] // 2
    return jnp.concatenate([v[:, :half] for v in pairs] + [v[:, half:] for v in pairs], axis=1)


def exchange_y(values, rider=None):
    rows, part = values.shape[0], values.shape[1] // 8
    sends = [
        jnp.concatenate(
            [
                values[:, p * part : (p + 1) * part],
                values[:, (4 + p) * part : (5 + p) * part],
            ],
            axis=1,
        ).astype(jnp.bfloat16)
        for p in range(4)
    ]
    if rider is not None:
        load = packed(rider, 2 * part)
        sends = [jnp.concatenate([v, load], axis=0) for v in sends]
    got = lax.all_to_all(jnp.stack(sends), "y", 0, 0)
    total = jnp.sum(got[:, :rows].astype(jnp.float32), axis=0)
    if rider is None:
        return total
    return total, sum(unpacked(got[i, rows:], rider.shape) for i in range(4))


def packed(values, columns):
    flat = values.reshape(-1)
    high, low = split(jnp.pad(flat, (0, -flat.size % columns)).reshape(-1, columns))
    both = jnp.concatenate([high, low], axis=0)
    return jnp.pad(both, ((0, -both.shape[0] % 16), (0, 0)))


def unpacked(block, shape):
    size = math.prod(shape)
    count = -(-size // block.shape[1])
    both = block[:count].astype(jnp.float32) + block[count : 2 * count].astype(jnp.float32)
    return both.reshape(-1)[:size].reshape(shape)


def scatter_y(values, bits):
    part = values.shape[1] // 8
    pairs = [
        jnp.concatenate(
            [
                values[:, p * part : (p + 1) * part],
                values[:, (4 + p) * part : (5 + p) * part],
            ],
            axis=1,
        )
        for p in range(4)
    ]
    mine = butterfly(pairs, bits)
    total = mine[0]
    for k in (1, 2, 3):
        total = total + swap(mine[k].astype(jnp.bfloat16), "y", k).astype(jnp.float32)
    return total


def devices(mask):
    return lambda values: swap(values, every, mask)


z_masks, x_masks, core_mask = (4, 8, 12), (16, 1, 17), 2


def gather_wide(values, xbits, zbits, core):
    columns = values.shape[1]
    along_x = jnp.stack(butterfly([values] + [devices(m)(values) for m in x_masks], xbits))
    along_z = butterfly([along_x] + [devices(m)(along_x) for m in z_masks], zbits)
    mine = jnp.stack(along_z, axis=1)
    across = devices(core_mask)(mine)
    both = jnp.stack(
        [jnp.where(core == 0, mine, across), jnp.where(core == 0, across, mine)], axis=2
    )
    return both.reshape(2, -1, columns)


def pick(values, index, axis):
    return lax.dynamic_index_in_dim(values, index, axis, keepdims=False)


def stage_sends(held, index, axis):
    sends = [pick(held, index ^ k, axis).astype(jnp.bfloat16) for k in (1, 2, 3)]
    return pick(held, index, axis).astype(jnp.float32), sends


def stage_arrive(sends, masks):
    return [devices(m)(v) for m, v in zip(masks, sends)]


def total_of(own, arrived):
    return own + sum(v.astype(jnp.float32) for v in arrived)


def ride(rider, masks):
    return rider + sum(devices(m)(rider) for m in masks)


def split(values):
    high = lax.reduce_precision(values, 8, 7)
    return high.astype(jnp.bfloat16), (values - high).astype(jnp.bfloat16)


def feed_kernel(rows, second, cot, grad0, grad1, act0, act1, out):
    width = out.shape[1]
    for s, (grad, act) in enumerate(((grad0, act0), (grad1, act1))):
        for j in range(3):

            @pl.when((pl.program_id(0) == s) & (pl.program_id(1) == j))
            def _():
                left = second if j < 2 else cot
                right = grad[:rows, j * width : (j + 1) * width] if j < 2 else act[:rows, :]
                out[...] = inner(left[:rows, :], right).astype(out.dtype)


def feed_wgrads(rows, second, cot, grads, acts):
    features, width = second.shape[1], acts[0].shape[1]
    operands = (second, cot, *grads, *acts)
    return pl.pallas_call(
        functools.partial(feed_kernel, rows),
        grid=(2, 3),
        in_specs=[pl.BlockSpec(v.shape, lambda s, j: (0, 0)) for v in operands],
        out_specs=pl.BlockSpec((features, width), lambda s, j: (s, j)),
        out_shape=pltpu.HBM((2 * features, 3 * width), jnp.bfloat16),
        compiler_params=pltpu.CompilerParams(vmem_limit_bytes=24 * 2**20),
        cost_estimate=pl.CostEstimate(
            flops=12 * rows * features * width,
            bytes_accessed=2 * sum(v.size for v in operands) + 12 * features * width,
            transcendentals=0,
        ),
    )(*operands)


def wgrad_kernel(rows, plan, summed, core, *refs):
    count = 2 if summed is None else 3
    operands, (send, held, *sums) = refs[:-count], refs[-count:]
    for s, line in enumerate(plan):
        for j, parts in enumerate(line):

            @pl.when((pl.program_id(0) == s) & (pl.program_id(1) == j))
            def _():
                at = 0
                for left, row, right, column, width in parts:
                    product = inner(
                        operands[left][row : row + rows, :],
                        operands[right][:rows, column : column + width],
                    )
                    if sums and at == 0:
                        terms = product * operands[summed + s][...].astype(jnp.float32)
                        terms = sum(terms[:, c : c + 128] for c in range(0, width, 128))
                        sums[0][...] = terms if s == 0 else sums[0][...] + terms
                    product = product.astype(send.dtype)
                    for b in range(8):
                        first = product[128 * b : 128 * b + 64]
                        second = product[128 * b + 64 : 128 * (b + 1)]
                        to = (slice(64 * b, 64 * (b + 1)), slice(at, at + width))
                        send[to] = jnp.where(core[0] == 0, second, first)
                        held[to] = jnp.where(core[0] == 0, first, second)
                    at += width


def wgrads(rows, plan, core, operands, summed=None, weight=1):
    features = operands[plan[0][0][0][0]].shape[1]
    width = sum(part[4] for part in plan[0][0])
    columns = width * len(plan[0])
    shape = jax.ShapeDtypeStruct((features, columns), jnp.bfloat16)
    block = pl.BlockSpec((features // 2, width), lambda s, j, c: (s, j))
    blocks, shapes = [block, block], [shape, shape]
    if summed is not None:
        blocks.append(pl.BlockSpec((features, 128), lambda s, j, c: (0, 0)))
        shapes.append(jax.ShapeDtypeStruct((features, 128), jnp.float32))
    return pl.pallas_call(
        functools.partial(wgrad_kernel, rows, plan, summed),
        grid_spec=pltpu.PrefetchScalarGridSpec(
            num_scalar_prefetch=1,
            grid=(2, len(plan[0])),
            in_specs=[pl.BlockSpec(v.shape, lambda s, j, c: (0, 0)) for v in operands],
            out_specs=blocks,
        ),
        out_shape=shapes,
        compiler_params=pltpu.CompilerParams(vmem_limit_bytes=24 * 2**20),
        cost_estimate=pl.CostEstimate(
            flops=weight * 4 * rows * features * columns,
            bytes_accessed=weight * (2 * sum(v.size for v in operands) + 4 * features * columns),
            transcendentals=0,
        ),
    )(core.reshape(1), *operands)


def windows(values, before, after):
    rows = values.shape[0] // 2
    padded = jnp.pad(values, ((before, after), (0, 0)))
    size = before + rows + after
    return padded[:size], padded[rows : rows + size]


def halves(own, got, h):
    return jnp.concatenate([jnp.where(h == 0, own, got), jnp.where(h == 0, got, own)], axis=1)


def body(
    tokens,
    segment_ids,
    mixer_gain,
    input_weight,
    filter_weight,
    output_weight,
    feed_gain,
    gate_weight,
    up_weight,
    down_weight,
    cotangent,
):
    h = lax.axis_index("xh")
    y = lax.axis_index("y")
    ybits = [(y & 1) == 1, (y & 2) == 2]
    place = lax.axis_index("dp")
    core = place & 1
    z = (place // 2) & 3
    x = place // 8 + 2 * h
    zbits = [(z & 1) == 1, (z & 2) == 2]
    xbits = [(x & 1) == 1, (x & 2) == 2]
    length, channels = tokens.shape
    rows = length // 2
    owned_rows = input_weight.shape[0]
    features = owned_rows * lax.axis_size("dp")
    hidden = gate_weight.shape[1]
    padded_hidden = -(-hidden // 128) * 128
    lanes = ((0, 0), (0, padded_hidden - hidden))
    taps = filter_weight.shape[0]
    f32, bf16 = jnp.float32, jnp.bfloat16

    mix_local = jnp.concatenate(
        [input_weight.reshape(owned_rows, 3 * channels), output_weight.T], axis=1
    )
    small = [split(v) for v in (mixer_gain, feed_gain)] + [split(filter_weight[i]) for i in range(taps)]
    small = jnp.stack([part for pair in small for part in pair])
    small = jnp.pad(small, ((0, extra - small.shape[0]), (0, 0)))
    first, second = windows(tokens, halo, halo)
    cot_first, cot_second = windows(cotangent, 0, halo)
    first = jnp.concatenate([small, first, cot_first], axis=0)
    second = jnp.concatenate([small, second, cot_second], axis=0)
    send = jnp.where(h == 0, second, first)
    own = jnp.where(h == 0, first, second)
    send, own, mix_local = lax.optimization_barrier((send, own, mix_local))
    gate_weight, send = lax.optimization_barrier((gate_weight, send))
    pair = halves(own, swap(send, "xh", 1), h)
    cot_at = extra + 2 * halo + rows
    tokens_pair, cot_pair = pair[:cot_at], pair[cot_at:]
    tokens_pair, cot_pair = pair[:cot_at], pair[cot_at:]
    tokens_full = natural(gather_y(tokens_pair, ybits))
    feed_local = jnp.concatenate(
        [jnp.pad(w, lanes) for w in (gate_weight, up_weight, down_weight.T)], axis=1
    )
    feed_full = lax.all_gather(feed_local, wide, axis=0, tiled=True)
    mix_full = gather_wide(mix_local, xbits, zbits, core)
    feed_full = feed_full.reshape(2, features, 3 * padded_hidden)
    w_up_gate = [feed_full[s, :, : 2 * padded_hidden] for s in range(2)]
    w_down = [feed_full[s, :, 2 * padded_hidden :] for s in range(2)]

    mix_full, cot_pair = lax.optimization_barrier((mix_full, cot_pair))
    cot_full = natural(gather_y(cot_pair, ybits))
    w_in = [mix_full[s, :, : 3 * channels] for s in range(2)]
    w_out = jnp.concatenate([mix_full[s, :, 3 * channels :] for s in range(2)], axis=1)

    def joined(block, index):
        return block[2 * index].astype(f32) + block[2 * index + 1].astype(f32)

    small_full, tokens_full = tokens_full[:extra], tokens_full[extra:].astype(f32)
    small_own = tokens_pair[:extra]
    tokens_own = tokens_pair[extra + halo :].astype(f32)
    cot_own = cot_pair.astype(f32)
    mixer_full, feed_full_gain = joined(small_full, 0), joined(small_full, 1)
    mixer_own, feed_own = joined(small_own, 0), joined(small_own, 1)
    tap = [joined(small_own, 2 + i) for i in range(taps)]

    positions = jnp.arange(length)
    prev_one = jnp.concatenate([segment_ids[:1], segment_ids[:-1]])
    prev_two = jnp.concatenate([segment_ids[:2], segment_ids[:-2]])
    keep = jnp.stack(
        [
            jnp.where((positions >= 1) & (segment_ids == prev_one), 1.0, 0.0),
            jnp.where((positions >= 2) & (segment_ids == prev_two), 1.0, 0.0),
        ],
        axis=1,
    ).astype(f32)
    keep_first, keep_second = windows(keep, halo, halo)
    keep = jnp.where(h == 0, keep_first, keep_second)
    keep_one, keep_two = keep[:, :1], keep[:, 1:]

    inv_one = lax.rsqrt(jnp.mean(tokens_full * tokens_full, axis=1, keepdims=True) + eps)
    first_full = (tokens_full * inv_one * mixer_full).astype(bf16)
    projected = [dot(first_full, w) for w in w_in]

    def column(index):
        return jnp.concatenate(
            [p[:, index * channels : (index + 1) * channels] for p in projected], axis=1
        )

    input_gate, output_gate, conv_input = column(0), column(1), column(2)
    mixed = input_gate * conv_input
    pad_rows = jnp.zeros((2, mixed.shape[1]), f32)
    mixed_one = jnp.concatenate([pad_rows[:1], mixed[:-1]], axis=0) * keep_one
    mixed_two = jnp.concatenate([pad_rows, mixed[:-2]], axis=0) * keep_two
    conv_out = tap[2] * mixed + tap[1] * mixed_one + tap[0] * mixed_two
    late = slice(halo, None)
    gated = (output_gate[late] * conv_out[late]).astype(bf16)
    resid_own = tokens_own + scatter_y(against(gated, w_out), ybits)
    resid_send = resid_own.astype(bf16)
    resid_full = natural(gather_y(resid_send, ybits)).astype(f32)

    inv_two = lax.rsqrt(jnp.mean(resid_full * resid_full, axis=1, keepdims=True) + eps)
    normed_two = resid_full * inv_two
    second_full = (normed_two * feed_full_gain).astype(bf16)
    both = [dot(second_full, w) for w in w_up_gate]
    gate_value = [b[:, :padded_hidden] for b in both]
    up_value = [b[:, padded_hidden:] for b in both]
    gate_sigmoid = [jax.nn.sigmoid(g) for g in gate_value]
    activated = [(g * s * u).astype(bf16) for g, s, u in zip(gate_value, gate_sigmoid, up_value)]
    feed_out = sum(against(a[:rows], w) for a, w in zip(activated, w_down))

    activated_grad = [dot(cot_full, w) for w in w_down]
    both_grad = [
        jnp.concatenate([d * u * s * (1.0 + g * (1.0 - s)), d * g * s], axis=1).astype(bf16)
        for d, g, u, s in zip(activated_grad, gate_value, up_value, gate_sigmoid)
    ]
    feed_wgrad = feed_wgrads(rows, second_full, cot_full, both_grad, activated)
    second_part = sum(against(g, w) for g, w in zip(both_grad, w_up_gate))
    second_send = scatter_y(second_part, ybits).astype(bf16)
    feed_owned = lax.psum_scatter(feed_wgrad, wide, scatter_dimension=0, tiled=True)
    second_grad = natural(gather_y(second_send, ybits))
    second_grad, feed_out = lax.optimization_barrier((second_grad, feed_out))
    second_grad = second_grad.astype(f32)

    scaled = second_grad * feed_full_gain
    mean_two = jnp.mean(scaled * normed_two, axis=1, keepdims=True)
    resid_grad = cot_full.astype(f32) + inv_two * (scaled - normed_two * mean_two)
    second_own = second_send.astype(f32)
    normed_own = resid_send.astype(f32) * inv_two
    feed_gain_grad = jnp.sum((second_own * normed_own)[:rows], axis=0)
    resid_grad_own = cot_own + inv_two * (second_own * feed_own - normed_own * mean_two)

    resid_low = resid_grad.astype(bf16)
    gated_grad = dot(resid_low, w_out)
    conv_grad = gated_grad * output_gate[late]
    kept_one = conv_grad * keep_one[late]
    kept_two = conv_grad * keep_two[late]
    mixed_grad = (
        tap[2] * conv_grad[:rows]
        + tap[1] * kept_one[1 : rows + 1]
        + tap[0] * kept_two[2 : rows + 2]
    )
    inside = slice(halo, halo + rows)
    output_gate_grad = gated_grad[:rows] * conv_out[inside]
    conv_grad = conv_grad[:rows]
    filter_local = [
        jnp.sum(conv_grad * mixed_two[inside], axis=0),
        jnp.sum(conv_grad * mixed_one[inside], axis=0),
        jnp.sum(conv_grad * mixed[inside], axis=0),
    ]
    input_gate_grad = mixed_grad * conv_input[inside]
    conv_input_grad = mixed_grad * input_gate[inside]
    projected_grad = [
        jnp.concatenate(
            [
                v[:, s * channels : (s + 1) * channels]
                for v in (input_gate_grad, output_gate_grad, conv_input_grad)
            ],
            axis=1,
        ).astype(bf16)
        for s in range(2)
    ]
    row_sum = sum(
        jnp.sum(d.astype(f32) * p[inside], axis=1) for d, p in zip(projected_grad, projected)
    )
    plan = [
        [[(0, halo, 3 + t, 0, 3 * channels), (1, 0, 2, t * channels, channels)]]
        for t in range(2)
    ]
    mix_send, mix_held, gain_terms = wgrads(
        rows, plan, core, (first_full, resid_low, gated, *projected_grad, *w_in), 5, 40
    )
    mix_send, *projected_late = lax.optimization_barrier((mix_send, *projected_grad))
    mix_held = mix_held.astype(f32) + devices(core_mask)(mix_send).astype(f32)
    summed = jnp.concatenate([jnp.sum(gain_terms, axis=1) / mixer_full, feed_gain_grad, *filter_local])
    summed = ride(summed.reshape(-1, 2 * channels), (core_mask,))
    first_part = sum(against(d, w) for d, w in zip(projected_late, w_in))
    mix_own, sends = stage_sends(mix_held.reshape(4, 4, owned_rows, -1), x, 0)
    load = packed(summed, mix_own.shape[-1])
    sends = [jnp.concatenate([v.reshape(4 * owned_rows, -1), load], axis=0) for v in sends]
    first_part, mix_own, *sends = lax.optimization_barrier((first_part, mix_own, *sends))
    arrived = stage_arrive(sends, x_masks)
    late_own, row_sum = exchange_y(
        jnp.concatenate([first_part.astype(bf16), feed_out.astype(bf16)], axis=0),
        row_sum.reshape(-1, 128),
    )
    late_own, row_sum, *arrived = lax.optimization_barrier((late_own, row_sum, *arrived))
    first_own, block_own = late_own[:rows], resid_own[:rows] + late_own[rows:]
    mix_own = total_of(mix_own, [v[: 4 * owned_rows].reshape(mix_own.shape) for v in arrived])
    summed = total_of(summed, [unpacked(v[4 * owned_rows :], summed.shape) for v in arrived])
    mix_own, sends = stage_sends(mix_own, z, 0)
    load = packed(summed, mix_own.shape[1])
    arrived = stage_arrive([jnp.concatenate([v, load], axis=0) for v in sends], z_masks)
    mix_owned = total_of(mix_own, [v[:owned_rows] for v in arrived])
    summed = total_of(summed, [unpacked(v[owned_rows:], summed.shape) for v in arrived])
    gains = summed.reshape(-1, channels)
    place = 4 * h + y
    mixer_gain_grad = pick(gains, place, 0) + sum(
        swap(pick(gains, place ^ k, 0), "y", k) for k in (1, 2, 3)
    )
    summed = summed[4:]
    mean_one = row_sum.reshape(rows, 1) / features
    normed_one = tokens_own[:rows] * inv_one[inside]
    input_own = resid_grad_own[:rows] + inv_one[inside] * (
        first_own * mixer_own - normed_one * mean_one
    )
    half = jnp.concatenate([block_own, input_own], axis=0).astype(bf16)
    mine = jnp.where(h == 0, half[:, :channels], half[:, channels:])
    got = swap(jnp.where(h == 0, half[:, channels:], half[:, :channels]), "xh", 1)
    input_mine = jnp.where(h == 0, input_own[:, :channels], input_own[:, channels:])

    def ordered(own, other):
        return jnp.concatenate([jnp.where(h == 0, own, other), jnp.where(h == 0, other, own)], axis=0)

    block_out = ordered(mine[:rows], got[:rows])
    input_grad = ordered(input_mine, got[rows:].astype(f32))

    gate_owned, up_owned, down_owned = (
        feed_owned[:, t * padded_hidden : t * padded_hidden + hidden].astype(f32) for t in range(3)
    )
    down_owned = down_owned.T
    input_owned = mix_owned[:, : 3 * channels].reshape(owned_rows, 3, channels)
    output_owned = mix_owned[:, 3 * channels :].T
    summed = jnp.where(h == 0, summed[:, :channels], summed[:, channels:])
    return (
        block_out,
        input_grad,
        mixer_gain_grad,
        input_owned,
        summed[1:],
        output_owned,
        summed[0],
        gate_owned,
        up_owned,
        down_owned,
    )


def solution(mesh):
    shape = mesh.devices.shape
    fine = Mesh(mesh.devices.reshape(shape[0], 2, shape[1] // 2), ("dp", "xh", "y"))
    dp, mp = "dp", ("xh", "y")
    placed = (
        P(dp, mp),
        P(dp),
        P(mp),
        P(dp, None, mp),
        P(None, mp),
        P(mp, dp),
        P(mp),
        P(dp, mp),
        P(dp, mp),
        P(mp, dp),
        P(dp, mp),
    )
    return jax.shard_map(
        body,
        mesh=fine,
        in_specs=placed,
        out_specs=(
            P(dp, mp),
            P(dp, mp),
            P(mp),
            P(dp, None, mp),
            P(None, mp),
            P(mp, dp),
            P(mp),
            P(dp, mp),
            P(dp, mp),
            P(mp, dp),
        ),
        check_vma=False,
    )
```
